256 devices in a mesh: lon: 32 (over x_hi, z, core), ch: 8 (over x_lo, y).
Axes of the slice: x: 4 (x_hi: 2, x_lo: 2; x = x_hi * 2 + x_lo), y: 4, z: 8, core: 2. Of those that a mesh axis runs over, the one named last changes fastest.
Arguments:
- field_state: bfloat16 [1440, 512, 256], P('lon', 'ch'), may hold values from -6 to 6
- zonal_taps: bfloat16 [256, 1440], replicated, may hold values from -0.15625 to 0.15625
- channel_mix: bfloat16 [512, 512], replicated, may hold values from -0.25 to 0.25
- channel_bias: float32 [512], replicated, may hold values from -3 to 3
Outputs:
- activated: bfloat16 [1440, 512, 256], P('lon', 'ch')
The draws below stay inside these ranges and needn't reach their ends.
All inputs are finite; a program needn't handle non-finite values.
Results may differ from the reference program's by a relative error of at most 0.0047.
Values may be sent and summed in bfloat16 or wider, within the bound.
No kernel may reach another device: no remote copies, remote signals or barrier semaphores. Data moves between devices by JAX's collectives and lax.ppermute only.
A program may use at most 64 MiB of HBM per device.

```python
import jax
import jax.numpy as jnp
from jax import lax

C = 512
NLON = 1440
LAT = 256


def level_of(key, extent, cuts, low, top_value):
    level = 1.0
    for position, parts in cuts:
        draws = jax.random.uniform(jax.random.fold_in(jax.random.fold_in(key, 6), position), (parts,), jnp.float32, low / len(cuts), top_value / len(cuts))
        level = level * jnp.repeat(jnp.exp(draws), extent[position] // parts).reshape((-1,) + (1,) * (len(extent) - 1 - position))
    return level


def centred(rng, dims, scale, bound, split=(), held_as=jnp.bfloat16):
    drawn = scale * jax.random.normal(rng, dims, jnp.float32)
    if split:
        drawn = drawn * level_of(rng, dims, split, -0.22, 0.18)
    return jnp.clip(drawn, -bound, bound).astype(held_as)


def setup_inputs(seed: int = 0) -> dict:
    streams_of = jax.random.split(jax.random.key(seed), 5)
    return {
        "field_state": centred(streams_of[0], (NLON, C, LAT), 1.0, 6.0, ((0, 32), (1, 8))),
        "zonal_taps": centred(streams_of[1], (LAT, NLON), NLON ** -0.5, 0.15625),
        "channel_mix": centred(streams_of[2], (C, C), C ** -0.5, 0.25),
        "channel_bias": centred(streams_of[3], (C,), 0.5, 3.0, (), jnp.float32),
    }


def reference(field_state, zonal_taps, channel_mix, channel_bias):
    values = jnp.transpose(field_state.astype(jnp.float32), (2, 0, 1))
    filters = zonal_taps.astype(jnp.float32)
    spectrum = jnp.fft.rfft(values, axis=1) * jnp.fft.rfft(filters, axis=1)[:, :, None]
    filtered = jnp.fft.irfft(spectrum, n=NLON, axis=1).astype(jnp.float32).astype(jnp.bfloat16)

    def one_row(row_values):
        mixed = jnp.dot(row_values, channel_mix, preferred_element_type=jnp.float32) + channel_bias
        return jax.nn.silu(mixed).astype(jnp.bfloat16)

    result = lax.map(one_row, filtered)
    return jnp.transpose(result, (1, 2, 0))
```

```python
import jax
import jax.numpy as jnp
from jax import lax
from jax.experimental import pallas as pl
from jax.experimental.pallas import tpu as pltpu
from jax.sharding import PartitionSpec as P

HALF = 23
ROWS = 24
LIMIT = 40 * 1024 * 1024


def params():
    return pltpu.CompilerParams(vmem_limit_bytes=LIMIT)


def identity(n):
    rows = lax.broadcasted_iota(jnp.int32, (n, n), 0)
    columns = lax.broadcasted_iota(jnp.int32, (n, n), 1)
    return jnp.where(rows == columns, 1.0, 0.0).astype(jnp.bfloat16)


def times_transposed(a, b):
    return lax.dot_general(a, b, (((1,), (1,)), ((), ())), preferred_element_type=jnp.float32)


def pack_kernel(width, depth, x_ref, out_ref, wide):
    lats = x_ref.shape[1]
    eye = identity(lats)
    for r in range(HALF):
        low = x_ref[r * depth : (r + 1) * depth, :]
        if HALF + r < width:
            high = x_ref[(HALF + r) * depth : (HALF + r + 1) * depth, :]
        else:
            high = jnp.zeros_like(low)
        wide[pl.ds(r, lats, stride=ROWS), :] = times_transposed(eye, jnp.concatenate([low, high], 0))
    for r in range(HALF, ROWS):
        wide[pl.ds(r, lats, stride=ROWS), :] = jnp.zeros((lats, 2 * depth), jnp.float32)
    out_ref[...] = wide[...].astype(out_ref.dtype)


def unpack_kernel(width, depth, y_ref, out_ref, wide):
    lats = out_ref.shape[1]
    eye = identity(2 * depth)
    wide[...] = y_ref[...].astype(jnp.float32)
    for r in range(HALF):
        rows = wide[pl.ds(r, lats, stride=ROWS), :].astype(jnp.bfloat16)
        turned = times_transposed(eye, rows).astype(out_ref.dtype)
        out_ref[r * depth : (r + 1) * depth, :] = turned[:depth]
        if HALF + r < width:
            out_ref[(HALF + r) * depth : (HALF + r + 1) * depth, :] = turned[depth:]


def toeplitz_kernel(shifts_ref, out_ref):
    tall, long = out_ref.shape
    base = jnp.broadcast_to(shifts_ref[...].astype(jnp.float32), (tall, shifts_ref.shape[1]))
    rolled = pltpu.roll(base, 0, 1, stride=1, stride_axis=0)
    out_ref[...] = rolled[:, tall:].astype(out_ref.dtype)


def compute_kernel(lon_count, ch_count, width, length, x_ref, t_ref, mix_ref, bias_ref, out_ref, state, packed, result):
    channels = state.shape[1]
    tall = t_ref.shape[0]
    half_lanes = 64
    low = lax.broadcasted_iota(jnp.int32, (ROWS, 128), 1) < half_lanes
    for l in range(lon_count):
        for pair in range(ch_count // 2):
            at = (l * ch_count + 2 * pair) * ROWS
            first = x_ref[at : at + ROWS, :].astype(jnp.float32)
            second = x_ref[at + ROWS : at + 2 * ROWS, :].astype(jnp.float32)
            lanes = slice(pair * 128, (pair + 1) * 128)
            state[l * width : l * width + ROWS, lanes] = jnp.where(low, first, pltpu.roll(second, half_lanes, 1))
            state[l * width + HALF : l * width + HALF + ROWS, lanes] = jnp.where(
                low, pltpu.roll(first, half_lanes, 1), second
            )
    padded = state.shape[0]
    packed[...] = state[...].astype(jnp.bfloat16)
    packed[length:, :] = jnp.zeros((padded - length, channels), jnp.bfloat16)
    result[length:, :] = jnp.zeros((result.shape[0] - length, channels), jnp.float32)
    blocks = (length + tall - 1) // tall
    for block in range(blocks):
        start = block * tall
        count = min(tall, length - start)
        offset = (length // 128) * 128 - start
        taps = t_ref[:count, offset : offset + padded]
        filtered = jnp.dot(taps, packed[...], preferred_element_type=jnp.float32).astype(jnp.bfloat16)
        mixed = jnp.dot(filtered, mix_ref[...], preferred_element_type=jnp.float32) + bias_ref[...]
        result[start : start + count, :] = mixed / (1.0 + jnp.exp(-mixed))
    for l in range(lon_count):
        for pair in range(ch_count // 2):
            lanes = slice(pair * 128, (pair + 1) * 128)
            first = result[l * width : l * width + ROWS, lanes]
            second = result[l * width + HALF : l * width + HALF + ROWS, lanes]
            at = (l * ch_count + 2 * pair) * ROWS
            out_ref[at : at + ROWS, :] = jnp.where(low, first, pltpu.roll(second, half_lanes, 1)).astype(out_ref.dtype)
            out_ref[at + ROWS : at + 2 * ROWS, :] = jnp.where(low, pltpu.roll(first, half_lanes, 1), second).astype(
                out_ref.dtype
            )


def exchange(x):
    return lax.all_to_all(x, ("lon", "ch"), split_axis=0, concat_axis=0, tiled=True)


def body(field_state, zonal_taps, channel_mix, channel_bias):
    lon_count = lax.axis_size("lon")
    ch_count = lax.axis_size("ch")
    width, depth, lats = field_state.shape
    length = zonal_taps.shape[1]
    channels = channel_mix.shape[0]
    tall = 256
    padded = -(-length // 128) * 128
    whole = (length // 128) * 128
    long = whole + padded
    sent = pl.pallas_call(
        lambda *refs: pack_kernel(width, depth, *refs),
        out_shape=jax.ShapeDtypeStruct((lats * ROWS, 2 * depth), jnp.bfloat16),
        scratch_shapes=[pltpu.VMEM((lats * ROWS, 2 * depth), jnp.float32)],
        compiler_params=params(),
        name="pack",
    )(field_state.reshape(width * depth, lats))
    mine = lax.axis_index("lon") * ch_count + lax.axis_index("ch")
    row = lax.dynamic_slice_in_dim(zonal_taps, mine, 1, 0)
    turned = jnp.flip(row, 1)
    start = (length - 1 - whole - tall) % length
    shifts = jnp.concatenate([turned[:, start:], turned, turned, turned], 1)[:, : long + tall]
    strip = pl.pallas_call(
        toeplitz_kernel,
        out_shape=jax.ShapeDtypeStruct((tall, long), jnp.bfloat16),
        compiler_params=params(),
        name="toeplitz",
    )(shifts)
    got = exchange(sent.reshape(lats, ROWS, 2 * depth)).reshape(lats * ROWS, 2 * depth)
    answer = pl.pallas_call(
        lambda *refs: compute_kernel(lon_count, ch_count, width, length, *refs),
        out_shape=jax.ShapeDtypeStruct((lats * ROWS, 2 * depth), jnp.bfloat16),
        scratch_shapes=[
            pltpu.VMEM((padded, channels), jnp.float32),
            pltpu.VMEM((padded, channels), jnp.bfloat16),
            pltpu.VMEM((padded, channels), jnp.float32),
        ],
        compiler_params=params(),
        name="filter_mix",
    )(got, strip, channel_mix, channel_bias.reshape(1, channels))
    back = exchange(answer.reshape(lats, ROWS, 2 * depth)).reshape(lats * ROWS, 2 * depth)
    out = pl.pallas_call(
        lambda *refs: unpack_kernel(width, depth, *refs),
        out_shape=jax.ShapeDtypeStruct((width * depth, lats), jnp.bfloat16),
        scratch_shapes=[pltpu.VMEM((lats * ROWS, 2 * depth), jnp.float32)],
        compiler_params=params(),
        name="unpack",
    )(back)
    return out.reshape(width, depth, lats)


def solution(mesh):
    placed = (P("lon", "ch", None), P(), P(), P())
    return jax.shard_map(
        body, mesh=mesh, in_specs=placed, out_specs=P("lon", "ch", None), check_vma=False
    )
```

```python
import jax
import jax.numpy as jnp
from jax import lax
from jax.experimental import pallas as pl
from jax.experimental.pallas import tpu as pltpu
from jax.sharding import PartitionSpec as P

HALF = 23
ROWS = 24
TALL = 256
LIMIT = 40 * 1024 * 1024
PIECES = 4


def params():
    return pltpu.CompilerParams(vmem_limit_bytes=LIMIT)


def identity(n):
    rows = lax.broadcasted_iota(jnp.int32, (n, n), 0)
    columns = lax.broadcasted_iota(jnp.int32, (n, n), 1)
    return jnp.where(rows == columns, 1.0, 0.0).astype(jnp.bfloat16)


def times_transposed(a, b):
    return lax.dot_general(a, b, (((1,), (1,)), ((), ())), preferred_element_type=jnp.float32)


def padded_length(length):
    return -(-length // 128) * 128


def strip_width(length):
    return (length // 128) * 128 + padded_length(length)


def periodic_reversed(row, length):
    padded = padded_length(length)
    whole = (length // 128) * 128
    chunks = padded // 128
    stacked = jnp.concatenate([row[:, c * 128 : (c + 1) * 128] for c in range(chunks)], 0)
    i = lax.broadcasted_iota(jnp.int32, (128, 128), 0)
    j = lax.broadcasted_iota(jnp.int32, (128, 128), 1)
    swap = jnp.where(i + j == 127, 1.0, 0.0).astype(jnp.bfloat16)
    flipped = jnp.dot(stacked.astype(jnp.bfloat16), swap, preferred_element_type=jnp.float32)
    width = strip_width(length) + TALL
    pieces = [flipped[c : c + 1, :] for c in range(chunks - 1, -1, -1)]
    pieces.append(jnp.zeros((1, width - padded), jnp.float32))
    line = jnp.broadcast_to(jnp.concatenate(pieces, 1), (8, width))
    column = lax.broadcasted_iota(jnp.int32, (8, width), 1)
    first = (whole + TALL + 1) % length - length
    result = jnp.zeros((8, width), jnp.float32)
    for start in range(first, width, length):
        shift = (start - (padded - length)) % width
        inside = (column >= start) & (column < start + length)
        result = jnp.where(inside, pltpu.roll(line, shift, 1), result)
    return result


def pack_kernel(width, depth, x_ref, out_ref, wide):
    lats = x_ref.shape[1]
    eye = identity(lats)
    for r in range(HALF):
        low = x_ref[r * depth : (r + 1) * depth, :]
        if HALF + r < width:
            high = x_ref[(HALF + r) * depth : (HALF + r + 1) * depth, :]
        else:
            high = jnp.zeros_like(low)
        wide[pl.ds(r, lats, stride=ROWS), :] = times_transposed(eye, jnp.concatenate([low, high], 0))
    for r in range(HALF, ROWS):
        wide[pl.ds(r, lats, stride=ROWS), :] = jnp.zeros((lats, 2 * depth), jnp.float32)
    out_ref[...] = wide[...].astype(out_ref.dtype)


def unpack_kernel(width, depth, y_ref, out_hbm, out_ref, wide, sems):
    lats = out_ref.shape[1]
    eye = identity(2 * depth)
    wide[...] = y_ref[...].astype(jnp.float32)
    step = -(-HALF // PIECES)
    copies = []
    for p in range(PIECES):
        a, b = min(p * step, HALF), min((p + 1) * step, HALF)
        for r in range(a, b):
            rows = wide[pl.ds(r, lats, stride=ROWS), :].astype(jnp.bfloat16)
            turned = times_transposed(eye, rows).astype(out_ref.dtype)
            out_ref[r * depth : (r + 1) * depth, :] = turned[:depth]
            if HALF + r < width:
                out_ref[(HALF + r) * depth : (HALF + r + 1) * depth, :] = turned[depth:]
        for side in range(2):
            rows = slice((side * HALF + a) * depth, min(side * HALF + b, width) * depth)
            copy = pltpu.make_async_copy(out_ref.at[rows, :], out_hbm.at[rows, :], sems.at[2 * p + side])
            copy.start()
            copies.append(copy)
    for copy in copies:
        copy.wait()


def filter_kernel(
    lon_count, ch_count, width, length, x_ref, turned_ref, mix_ref, bias_ref, out_ref, strip, state, packed, result
):
    channels = state.shape[1]
    half_lanes = 64
    me = lax.axis_index("lon") * ch_count + lax.axis_index("ch")
    chosen = lax.broadcasted_iota(jnp.int32, (16, turned_ref.shape[1]), 1) == me
    row = times_transposed(jnp.where(chosen, 1.0, 0.0).astype(jnp.bfloat16), turned_ref[...])[0:1]
    row = jnp.concatenate([row, jnp.zeros((1, padded_length(length) - length), jnp.float32)], 1)
    line = periodic_reversed(row, length)
    base = jnp.broadcast_to(line[0:1, :], (TALL, line.shape[1]))
    strip[...] = pltpu.roll(base, 0, 1, stride=1, stride_axis=0)[:, TALL:].astype(strip.dtype)
    low = lax.broadcasted_iota(jnp.int32, (ROWS, 128), 1) < half_lanes
    for l in range(lon_count):
        for pair in range(ch_count // 2):
            at = (l * ch_count + 2 * pair) * ROWS
            first = x_ref[at : at + ROWS, :].astype(jnp.float32)
            second = x_ref[at + ROWS : at + 2 * ROWS, :].astype(jnp.float32)
            lanes = slice(pair * 128, (pair + 1) * 128)
            state[l * width : l * width + ROWS, lanes] = jnp.where(low, first, pltpu.roll(second, half_lanes, 1))
            state[l * width + HALF : l * width + HALF + ROWS, lanes] = jnp.where(
                low, pltpu.roll(first, half_lanes, 1), second
            )
    padded = state.shape[0]
    packed[...] = state[...].astype(jnp.bfloat16)
    packed[length:, :] = jnp.zeros((padded - length, channels), jnp.bfloat16)
    result[length:, :] = jnp.zeros((result.shape[0] - length, channels), jnp.float32)
    for start in range(0, length, TALL):
        count = min(TALL, length - start)
        offset = (length // 128) * 128 - start
        taps = strip[:count, offset : offset + padded]
        filtered = jnp.dot(taps, packed[...], preferred_element_type=jnp.float32).astype(jnp.bfloat16)
        mixed = jnp.dot(filtered, mix_ref[...], preferred_element_type=jnp.float32) + bias_ref[...]
        result[start : start + count, :] = mixed / (1.0 + jnp.exp(-mixed))
    for l in range(lon_count):
        for pair in range(ch_count // 2):
            lanes = slice(pair * 128, (pair + 1) * 128)
            first = result[l * width : l * width + ROWS, lanes]
            second = result[l * width + HALF : l * width + HALF + ROWS, lanes]
            at = (l * ch_count + 2 * pair) * ROWS
            out_ref[at : at + ROWS, :] = jnp.where(low, first, pltpu.roll(second, half_lanes, 1)).astype(out_ref.dtype)
            out_ref[at + ROWS : at + 2 * ROWS, :] = jnp.where(low, pltpu.roll(first, half_lanes, 1), second).astype(
                out_ref.dtype
            )


def exchange(x):
    return lax.all_to_all(x, ("lon", "ch"), split_axis=0, concat_axis=0, tiled=True)


def pack(field, width, depth):
    lats = field.shape[1]
    return pl.pallas_call(
        lambda *refs: pack_kernel(width, depth, *refs),
        out_shape=jax.ShapeDtypeStruct((lats * ROWS, 2 * depth), jnp.bfloat16),
        scratch_shapes=[pltpu.VMEM((lats * ROWS, 2 * depth), jnp.float32)],
        compiler_params=params(),
        name="pack",
    )(field)


def filter_mix(got, zonal_taps, channel_mix, channel_bias, lon_count, ch_count, width):
    channels = channel_mix.shape[0]
    length = zonal_taps.shape[1]
    padded = padded_length(length)
    return pl.pallas_call(
        lambda *refs: filter_kernel(lon_count, ch_count, width, length, *refs),
        out_shape=jax.ShapeDtypeStruct(got.shape, jnp.bfloat16),
        scratch_shapes=[
            pltpu.VMEM((TALL, strip_width(length)), jnp.bfloat16),
            pltpu.VMEM((padded, channels), jnp.float32),
            pltpu.VMEM((padded, channels), jnp.bfloat16),
            pltpu.VMEM((padded, channels), jnp.float32),
        ],
        compiler_params=params(),
        name="filter_mix",
    )(got, zonal_taps.T, channel_mix, channel_bias.reshape(1, channels))


def unpack(back, width, depth, lats):
    return pl.pallas_call(
        lambda *refs: unpack_kernel(width, depth, *refs),
        out_shape=jax.ShapeDtypeStruct((width * depth, lats), jnp.bfloat16),
        out_specs=pl.BlockSpec(memory_space=pltpu.HBM),
        scratch_shapes=[
            pltpu.VMEM((width * depth, lats), jnp.bfloat16),
            pltpu.VMEM((lats * ROWS, 2 * depth), jnp.float32),
            pltpu.SemaphoreType.DMA((2 * PIECES,)),
        ],
        compiler_params=params(),
        name="unpack",
    )(back)


def body(field_state, zonal_taps, channel_mix, channel_bias):
    lon_count = lax.axis_size("lon")
    ch_count = lax.axis_size("ch")
    width, depth, lats = field_state.shape
    sent = pack(field_state.reshape(width * depth, lats), width, depth)
    got = exchange(sent.reshape(lats, ROWS, 2 * depth)).reshape(sent.shape)
    answer = filter_mix(got, zonal_taps, channel_mix, channel_bias, lon_count, ch_count, width)
    back = exchange(answer.reshape(lats, ROWS, 2 * depth)).reshape(sent.shape)
    return unpack(back, width, depth, lats).reshape(width, depth, lats)


def solution(mesh):
    placed = (P("lon", "ch", None), P(), P(), P())
    return jax.shard_map(
        body, mesh=mesh, in_specs=placed, out_specs=P("lon", "ch", None), check_vma=False
    )
```

```python
import jax
import jax.numpy as jnp
from jax import lax
from jax.experimental import pallas as pl
from jax.experimental.pallas import tpu as pltpu
from jax.sharding import PartitionSpec as P

HALF = 23
ROWS = 24
TALL = 384
LIMIT = 40 * 1024 * 1024
PIECES = 6


def params():
    return pltpu.CompilerParams(vmem_limit_bytes=LIMIT)


def identity(n):
    rows = lax.broadcasted_iota(jnp.int32, (n, n), 0)
    columns = lax.broadcasted_iota(jnp.int32, (n, n), 1)
    return jnp.where(rows == columns, 1.0, 0.0).astype(jnp.bfloat16)


def times_transposed(a, b):
    return lax.dot_general(a, b, (((1,), (1,)), ((), ())), preferred_element_type=jnp.float32)


def padded_length(length):
    return -(-length // 128) * 128


def strip_width(length):
    return (length // 128) * 128 + padded_length(length)


def periodic_reversed(row, length):
    padded = padded_length(length)
    whole = (length // 128) * 128
    chunks = padded // 128
    stacked = jnp.concatenate([row[:, c * 128 : (c + 1) * 128] for c in range(chunks)], 0)
    i = lax.broadcasted_iota(jnp.int32, (128, 128), 0)
    j = lax.broadcasted_iota(jnp.int32, (128, 128), 1)
    swap = jnp.where(i + j == 127, 1.0, 0.0).astype(jnp.bfloat16)
    flipped = jnp.dot(stacked.astype(jnp.bfloat16), swap, preferred_element_type=jnp.float32)
    width = strip_width(length) + TALL
    pieces = [flipped[c : c + 1, :] for c in range(chunks - 1, -1, -1)]
    pieces.append(jnp.zeros((1, width - padded), jnp.float32))
    line = jnp.broadcast_to(jnp.concatenate(pieces, 1), (8, width))
    column = lax.broadcasted_iota(jnp.int32, (8, width), 1)
    first = (whole + TALL + 1) % length - length
    result = jnp.zeros((8, width), jnp.float32)
    for start in range(first, width, length):
        shift = (start - (padded - length)) % width
        inside = (column >= start) & (column < start + length)
        result = jnp.where(inside, pltpu.roll(line, shift, 1), result)
    return result


def pack_kernel(width, depth, x_ref, out_ref, wide):
    lats = x_ref.shape[1]
    eye = identity(lats)
    for r in range(HALF):
        low = x_ref[r * depth : (r + 1) * depth, :]
        if HALF + r < width:
            high = x_ref[(HALF + r) * depth : (HALF + r + 1) * depth, :]
        else:
            high = jnp.zeros_like(low)
        wide[pl.ds(r, lats, stride=ROWS), :] = times_transposed(eye, jnp.concatenate([low, high], 0))
    for r in range(HALF, ROWS):
        wide[pl.ds(r, lats, stride=ROWS), :] = jnp.zeros((lats, 2 * depth), jnp.float32)
    out_ref[...] = wide[...].astype(out_ref.dtype)


def unpack_kernel(width, depth, y_ref, out_hbm, out_ref, wide, sems):
    lats = out_ref.shape[1]
    eye = identity(2 * depth)
    wide[...] = y_ref[...].astype(jnp.float32)
    step = -(-HALF // PIECES)
    copies = []
    for p in range(PIECES):
        a, b = min(p * step, HALF), min((p + 1) * step, HALF)
        for r in range(a, b):
            rows = wide[pl.ds(r, lats, stride=ROWS), :].astype(jnp.bfloat16)
            turned = times_transposed(eye, rows).astype(out_ref.dtype)
            out_ref[r * depth : (r + 1) * depth, :] = turned[:depth]
            if HALF + r < width:
                out_ref[(HALF + r) * depth : (HALF + r + 1) * depth, :] = turned[depth:]
        for side in range(2):
            rows = slice((side * HALF + a) * depth, min(side * HALF + b, width) * depth)
            copy = pltpu.make_async_copy(out_ref.at[rows, :], out_hbm.at[rows, :], sems.at[2 * p + side])
            copy.start()
            copies.append(copy)
    for copy in copies:
        copy.wait()


def filter_kernel(
    lon_count, ch_count, width, length, x_ref, turned_ref, mix_ref, bias_ref, out_ref, strip, state, packed, result, half
):
    channels = state.shape[1]
    half_lanes = 64
    me = lax.axis_index("lon") * ch_count + lax.axis_index("ch")
    chosen = lax.broadcasted_iota(jnp.int32, (16, turned_ref.shape[1]), 1) == me
    row = times_transposed(jnp.where(chosen, 1.0, 0.0).astype(jnp.bfloat16), turned_ref[...])[0:1]
    row = jnp.concatenate([row, jnp.zeros((1, padded_length(length) - length), jnp.float32)], 1)
    line = periodic_reversed(row, length)
    base = jnp.broadcast_to(line[0:1, :], (TALL, line.shape[1]))
    strip[...] = pltpu.roll(base, 0, 1, stride=1, stride_axis=0)[:, TALL:].astype(strip.dtype)
    low = lax.broadcasted_iota(jnp.int32, (ROWS, 128), 1) < half_lanes
    padded = state.shape[0]
    pairs = ch_count // 2
    sides = [slice(0, channels // 2), slice(channels // 2, channels)]

    def take(l, side):
        for pair in range(side * pairs // 2, (side + 1) * pairs // 2):
            at = (l * ch_count + 2 * pair) * ROWS
            first = x_ref[at : at + ROWS, :].astype(jnp.float32)
            second = x_ref[at + ROWS : at + 2 * ROWS, :].astype(jnp.float32)
            lanes = slice(pair * 128, (pair + 1) * 128)
            state[l * width : l * width + ROWS, lanes] = jnp.where(low, first, pltpu.roll(second, half_lanes, 1))
            state[l * width + HALF : l * width + HALF + ROWS, lanes] = jnp.where(
                low, pltpu.roll(first, half_lanes, 1), second
            )

    def close(side):
        packed[:length, sides[side]] = state[:length, sides[side]].astype(jnp.bfloat16)
        packed[length:, sides[side]] = jnp.zeros((padded - length, channels // 2), jnp.bfloat16)

    def filtered_block(block, side):
        start, count = block
        offset = (length // 128) * 128 - start
        taps = strip[:count, offset : offset + padded]
        return jnp.dot(taps, packed[:, sides[side]], preferred_element_type=jnp.float32).astype(jnp.bfloat16)

    for l in range(lon_count):
        take(l, 0)
    close(0)
    result[length:, :] = jnp.zeros((result.shape[0] - length, channels), jnp.float32)

    def finish(start, filtered):
        mixed = jnp.dot(filtered, mix_ref[...], preferred_element_type=jnp.float32) + bias_ref[...]
        result[start : start + filtered.shape[0], :] = mixed / (1.0 + jnp.exp(-mixed))

    def send(l):
        for pair in range(ch_count // 2):
            lanes = slice(pair * 128, (pair + 1) * 128)
            first = result[l * width : l * width + ROWS, lanes]
            second = result[l * width + HALF : l * width + HALF + ROWS, lanes]
            at = (l * ch_count + 2 * pair) * ROWS
            out_ref[at : at + ROWS, :] = jnp.where(low, first, pltpu.roll(second, half_lanes, 1)).astype(out_ref.dtype)
            out_ref[at + ROWS : at + 2 * ROWS, :] = jnp.where(low, pltpu.roll(first, half_lanes, 1), second).astype(
                out_ref.dtype
            )

    blocks = [(start, min(TALL, length - start)) for start in range(0, length, TALL)]
    taken = 0
    for i, block in enumerate(blocks):
        half[block[0] : block[0] + block[1], :] = filtered_block(block, 0)
        upto = lon_count * (i + 1) // len(blocks)
        for l in range(taken, upto):
            take(l, 1)
        taken = upto
    close(1)
    waiting = None
    sent = 0
    for stage in range(len(blocks) + 2):
        if stage < len(blocks):
            start, count = blocks[stage]
            latest = jnp.concatenate([half[start : start + count, :], filtered_block(blocks[stage], 1)], 1)
        if 1 <= stage <= len(blocks):
            finish(blocks[stage - 1][0], waiting)
        waiting = latest
        if stage >= 2:
            known = blocks[stage - 2][0] + blocks[stage - 2][1]
            while sent < lon_count and (known >= length or sent * width + HALF + ROWS <= known):
                send(sent)
                sent += 1


def exchange(x):
    return lax.all_to_all(x, ("lon", "ch"), split_axis=0, concat_axis=0, tiled=True)


def pack(field, width, depth):
    lats = field.shape[1]
    return pl.pallas_call(
        lambda *refs: pack_kernel(width, depth, *refs),
        out_shape=jax.ShapeDtypeStruct((lats * ROWS, 2 * depth), jnp.bfloat16),
        scratch_shapes=[pltpu.VMEM((lats * ROWS, 2 * depth), jnp.float32)],
        compiler_params=params(),
        name="pack",
    )(field)


def filter_mix(got, zonal_taps, channel_mix, channel_bias, lon_count, ch_count, width):
    channels = channel_mix.shape[0]
    length = zonal_taps.shape[1]
    padded = padded_length(length)
    return pl.pallas_call(
        lambda *refs: filter_kernel(lon_count, ch_count, width, length, *refs),
        out_shape=jax.ShapeDtypeStruct(got.shape, jnp.bfloat16),
        scratch_shapes=[
            pltpu.VMEM((TALL, strip_width(length)), jnp.bfloat16),
            pltpu.VMEM((padded, channels), jnp.float32),
            pltpu.VMEM((padded, channels), jnp.bfloat16),
            pltpu.VMEM((padded, channels), jnp.float32),
            pltpu.VMEM((padded, channels // 2), jnp.bfloat16),
        ],
        compiler_params=params(),
        name="filter_mix",
    )(got, zonal_taps.T, channel_mix, channel_bias.reshape(1, channels))


def unpack(back, width, depth, lats):
    return pl.pallas_call(
        lambda *refs: unpack_kernel(width, depth, *refs),
        out_shape=jax.ShapeDtypeStruct((width * depth, lats), jnp.bfloat16),
        out_specs=pl.BlockSpec(memory_space=pltpu.HBM),
        scratch_shapes=[
            pltpu.VMEM((width * depth, lats), jnp.bfloat16),
            pltpu.VMEM((lats * ROWS, 2 * depth), jnp.float32),
            pltpu.SemaphoreType.DMA((2 * PIECES,)),
        ],
        compiler_params=params(),
        name="unpack",
    )(back)


def body(field_state, zonal_taps, channel_mix, channel_bias):
    lon_count = lax.axis_size("lon")
    ch_count = lax.axis_size("ch")
    width, depth, lats = field_state.shape
    sent = pack(field_state.reshape(width * depth, lats), width, depth)
    got = exchange(sent.reshape(lats, ROWS, 2 * depth)).reshape(sent.shape)
    answer = filter_mix(got, zonal_taps, channel_mix, channel_bias, lon_count, ch_count, width)
    back = exchange(answer.reshape(lats, ROWS, 2 * depth)).reshape(sent.shape)
    return unpack(back, width, depth, lats).reshape(width, depth, lats)


def solution(mesh):
    placed = (P("lon", "ch", None), P(), P(), P())
    return jax.shard_map(
        body, mesh=mesh, in_specs=placed, out_specs=P("lon", "ch", None), check_vma=False
    )
```
